32 devices in a mesh: modes: 16 (over z, y, x), mom: 2 (over core).
Axes of the slice: x: 2, y: 2, z: 4, core: 2. Of those that a mesh axis runs over, the one named last changes fastest.
Arguments:
- elementals: float32 [2, 4, 256, 256, 256], P(None, 'mom', 'modes'), parts along dimension 1, may hold values from -64 to 64
- perambulators: float32 [16, 2, 2, 256, 256], P('modes'), may hold values from -0.25 to 0.25
- owners: int32 [2], replicated, may hold values from 0 to 15
- pairing: int32 [4], P('mom'), parts along dimension 0, may hold values from 0 to 1
Outputs:
- propagated: bfloat16 [2, 4, 2, 256, 256, 256], P(None, 'mom', None, 'modes'), parts along dimension 1
- correlator: float32 [2, 4, 2], P(None, 'mom'), parts along dimension 1
The draws below stay inside these ranges and needn't reach their ends.
There are 2 independent parts, one for each index of `mom`. The reference program is written for one: setup_inputs(seed, part) draws one part's arguments, and reference() takes and returns one part's arrays. A program takes and returns all parts, laid end to end along the dimension named above; an argument that names none is the same for every part. Nothing has to cross between parts.
All inputs are finite; a program needn't handle non-finite values.
Results may differ from the reference program's by a relative error of at most 0.001.
Values sent between devices are 32-bit elements; how exact they have to be, the bound alone decides.
A program may use at most 192 MiB of HBM per device.

```python
import jax
import jax.numpy as jnp
from jax import lax

N = 256
MOMS = 2
TIMES = 2
N_MODES = 16


def draw_elementals(key, part):
    base_key = jax.random.fold_in(jax.random.fold_in(key, 17), 0)
    full_shape = (2, MOMS, N, N, N)
    position_ramp = jnp.arange(N, dtype=jnp.float32) / max(N - 1, 1)
    values = jax.random.truncated_normal(base_key, -6.0, 6.0, full_shape, jnp.float32)
    rising = jnp.exp(jnp.log(3.0) * position_ramp)
    return values * rising[None, None, :, None, None]


def level_of(stream_key, extent, shards, smallest, top_value):
    factor_of, own = 1.0, jax.random.fold_in(stream_key, 6)
    for dim, blocks in shards:
        draws = jnp.exp(jax.random.uniform(jax.random.fold_in(own, dim), (blocks,), jnp.float32, smallest / len(shards), top_value / len(shards)))
        factor_of = factor_of * jnp.repeat(draws, extent[dim] // blocks).reshape([-1 if axis == dim else 1 for axis in range(len(extent))])
    return factor_of


def centred(key, extent, scale, reach, shards=(), held_as=jnp.bfloat16):
    result = jax.random.normal(key, extent, jnp.float32) * scale
    if len(shards) > 0:
        result = level_of(key, extent, shards, -0.22, 0.18) * result
    return jnp.clip(result, min=-reach, max=reach).astype(held_as)


def setup_inputs(seed: int = 0, part: int = 0) -> dict:
    arg_keys = jax.random.split(jax.random.key(seed), 5)
    part_splits = jax.random.split(jax.random.fold_in(arg_keys[4], part), 5)
    return {
        "elementals": draw_elementals(jax.random.fold_in(jax.random.fold_in(arg_keys[4], part), 71), part),
        "perambulators": centred(arg_keys[1], (N_MODES, TIMES, 2, N, N), (2 * N) ** -0.5, 0.25, ((0, 16),), jnp.float32),
        "owners": jax.random.randint(arg_keys[2], (TIMES,), 0, N_MODES).astype(jnp.int32),
        "pairing": jax.random.randint(part_splits[3], (MOMS,), 0, MOMS).astype(jnp.int32),
    }


highest = lax.Precision.HIGHEST


def complex_product(formula, matrix_re, matrix_im, tensor_re, tensor_im):
    def single(left_part, right_part):
        return jnp.einsum(formula, left_part, right_part, precision=highest)
    real_part = single(matrix_re, tensor_re) - single(matrix_im, tensor_im)
    imag_part = single(matrix_re, tensor_im) + single(matrix_im, tensor_re)
    return real_part, imag_part


def transform(elem_re, elem_im, peram_re, peram_im):
    third_re, third_im = complex_product("kc,abc->abk", peram_re, peram_im, elem_re, elem_im)
    second_re, second_im = complex_product("jb,abk->kaj", peram_re, peram_im, third_re, third_im)
    return complex_product("ia,kaj->kij", peram_re, peram_im, second_re, second_im)


def reference(elementals, perambulators, owners, pairing):
    norm_scale = float(N) ** -1.5
    sink_slabs = []
    for mom_index in range(MOMS):
        picked = lax.dynamic_index_in_dim(elementals, pairing[mom_index], 1, keepdims=False)
        sink_slabs.append((jnp.swapaxes(picked[0], 1, 2), jnp.swapaxes(picked[1], 1, 2)))
    real_rows = []
    imag_rows = []
    corr_real = []
    corr_imag = []
    for mom_index in range(MOMS):
        time_real = []
        time_imag = []
        sums_real = []
        sums_imag = []
        for time_index in range(TIMES):
            peram_now = lax.dynamic_index_in_dim(perambulators[:, time_index], owners[time_index], 0, keepdims=False)
            out_re, out_im = transform(elementals[0, mom_index], elementals[1, mom_index], peram_now[0], peram_now[1])
            sink_re, sink_im = sink_slabs[mom_index]
            sums_real.append(jnp.sum(sink_re * out_re + sink_im * out_im) * norm_scale)
            sums_imag.append(jnp.sum(sink_re * out_im - sink_im * out_re) * norm_scale)
            time_real.append(out_re)
            time_imag.append(out_im)
        real_rows.append(jnp.stack(time_real))
        imag_rows.append(jnp.stack(time_imag))
        corr_real.append(jnp.stack(sums_real))
        corr_imag.append(jnp.stack(sums_imag))
    propagated = jnp.stack([jnp.stack(real_rows), jnp.stack(imag_rows)]).astype(jnp.bfloat16)
    correlator = jnp.stack([jnp.stack(corr_real), jnp.stack(corr_imag)])
    return propagated, correlator
```

```python
import jax
import jax.numpy as jnp
from jax import lax
from jax.sharding import PartitionSpec as P

high = lax.Precision.HIGH


def scatter_pick_gather(perams, owners, mode_count, mom_count):
    times, parts, n = perams.shape[0], perams.shape[1], perams.shape[2]
    rows = parts * n
    both = rows % (8 * mode_count * mom_count) == 0
    pieces = mode_count * mom_count if both else mode_count
    names = ("modes", "mom") if both else "modes"
    flat = jnp.swapaxes(perams.reshape(times, pieces, rows // pieces, n), 0, 1)
    if both:
        flat = flat.reshape((mode_count, mom_count) + flat.shape[1:])
        flat = lax.dynamic_index_in_dim(flat, lax.axis_index("mom"), 1, keepdims=False)
    seen = lax.all_to_all(flat, "modes", split_axis=0, concat_axis=0, tiled=True)
    mine = jnp.stack(
        [lax.dynamic_index_in_dim(seen[:, t], owners[t], 0, keepdims=False) for t in range(times)]
    )
    spread_out = jnp.broadcast_to(mine[None], (pieces,) + mine.shape)
    whole = lax.all_to_all(spread_out, names, split_axis=0, concat_axis=0, tiled=True)
    return jnp.swapaxes(whole, 0, 1).reshape(times, parts, n, n)


def real_form(peram):
    re, im = peram[0], peram[1]
    return jnp.stack([jnp.stack([re, -im], axis=1), jnp.stack([im, re], axis=1)])


def before(elem, form, mode_count):
    third = jnp.einsum("PkCc,Cabc->Pabk", form, elem, precision=high)
    second = jnp.einsum("QjPb,Pabk->Qkaj", form, third, precision=high)
    comps, n, slab, _ = second.shape
    return jnp.moveaxis(second.reshape(comps, mode_count, n // mode_count, slab, n), 1, 0)


def after(arrived, form, mode_count):
    comps, n = form.shape[0], form.shape[1]
    split = form.reshape(comps, n, comps, mode_count, n // mode_count)
    return jnp.einsum("RiQsa,sQkaj->Rkij", split, arrived, precision=high)


def shards(mode_count, mom_count, elementals, perambulators, owners, pairing):
    momenta = elementals.shape[1]
    times = perambulators.shape[1]
    n = elementals.shape[-1]
    norm_scale = float(n) ** (-1.5)
    taus = scatter_pick_gather(perambulators[0], owners, mode_count, mom_count)
    forms = [real_form(taus[t]) for t in range(times)]
    steps = [(t, m) for t in range(times) for m in range(momenta)]
    slab = elementals.shape[2]
    out = jnp.zeros((2, momenta, times, slab, n, n), jnp.bfloat16)
    sums = {}

    def finish(step, arrived, out):
        t, m = step
        result = after(arrived, forms[t], mode_count)
        rounded = result.astype(jnp.bfloat16)[:, None, None]
        out = lax.dynamic_update_slice(out, rounded, (0, m, t, 0, 0, 0))
        sink = lax.dynamic_index_in_dim(elementals, pairing[m], 1, keepdims=False)
        sink = jnp.swapaxes(sink, 2, 3)
        real = jnp.sum(sink[0] * result[0] + sink[1] * result[1])
        imag = jnp.sum(sink[0] * result[1] - sink[1] * result[0])
        sums[step] = (real, imag)
        return out, real, imag

    waiting = None
    for index, (t, m) in enumerate(steps):
        elem, form = elementals[:, m], forms[t]
        if index >= 2:
            (out, real, imag), form = lax.optimization_barrier(
                (finish(steps[index - 2], waiting[index - 2], out), form)
            )
            sums[steps[index - 2]] = (real, imag)
        else:
            waiting = waiting or {}
        packed = before(elem, form, mode_count)
        waiting[index] = lax.all_to_all(packed, "modes", split_axis=0, concat_axis=0, tiled=True)
    for index in range(max(len(steps) - 2, 0), len(steps)):
        out, real, imag = finish(steps[index], waiting[index], out)

    partial = jnp.stack(
        [
            jnp.stack([jnp.stack([sums[(t, m)][c] for t in range(times)]) for m in range(momenta)])
            for c in range(2)
        ]
    )
    shares = jnp.broadcast_to(partial.reshape(1, 1, -1), (mode_count, 1, partial.size))
    shares = lax.all_to_all(shares, "modes", split_axis=0, concat_axis=0, tiled=True)
    correlator = jnp.sum(shares, axis=(0, 1)).reshape(partial.shape) * norm_scale
    return (out, correlator)


def solution(mesh):
    mode_count, mom_count = mesh.shape["modes"], mesh.shape["mom"]
    placed = (
        P(None, "mom", "modes", None, None),
        P("modes", None, None, None, None),
        P(),
        P("mom"),
    )

    def local(elementals, perambulators, owners, pairing):
        return shards(mode_count, mom_count, elementals, perambulators, owners, pairing)

    return jax.shard_map(
        local,
        mesh=mesh,
        in_specs=placed,
        out_specs=(P(None, "mom", None, "modes", None, None), P(None, "mom", None)),
        check_vma=False,
    )
```
